32 devices in a mesh: dp: 16 (over z, y, core), tensor: 2 (over x).
Axes of the slice: x: 2, y: 2, z: 4, core: 2. Of those that a mesh axis runs over, the one named last changes fastest.
Arguments:
- hidden_in: bfloat16 [7168, 1024], P('dp'), may hold values from -6 to 6
- segment_ids: int32 [16, 448], P('dp'), may hold values from 0 to 2, never falling along the last dimension, each value on 1 to 336 neighbouring positions
- attn_gain: float32 [1024], replicated, may hold values from 0.5 to 1.5
- w_query: bfloat16 [1024, 2048], P(None, 'tensor'), may hold values from -0.1875 to 0.1875
- key_projection: bfloat16 [1024, 1024], P(None, 'tensor'), may hold values from -0.1875 to 0.1875
- value_projection: bfloat16 [1024, 1024], P(None, 'tensor'), may hold values from -0.1875 to 0.1875
- query_gain: float32 [128], replicated, may hold values from 0.5 to 2
- key_gain: float32 [128], replicated, may hold values from 0.5 to 2
- w_out: bfloat16 [2048, 1024], P('tensor'), may hold values from -1 to 1
- mlp_gain: float32 [1024], replicated, may hold values from 0.5 to 1.5
- w_gate: bfloat16 [1024, 3072], P(None, 'tensor'), may hold values from -0.1875 to 0.1875
- w_up: bfloat16 [1024, 3072], P(None, 'tensor'), may hold values from -0.1875 to 0.1875
- w_down: bfloat16 [3072, 1024], P('tensor'), may hold values from -0.21875 to 0.21875
- cotangent: bfloat16 [7168, 1024], P(('dp', 'tensor')), may hold values from -6 to 6
Outputs:
- layer_output: bfloat16 [7168, 1024], P(('dp', 'tensor'))
- grad_in: float32 [7168, 1024], P(('dp', 'tensor'))
- attention_gain_gradient: float32 [1024], replicated
- grad_w_query: float32 [1024, 2048], P('dp', 'tensor')
- grad_w_key: float32 [1024, 1024], P('dp', 'tensor')
- grad_w_value: float32 [1024, 1024], P('dp', 'tensor')
- grad_query_gain: float32 [128], replicated
- grad_key_gain: float32 [128], replicated
- grad_w_out: float32 [2048, 1024], P('tensor', 'dp')
- grad_mlp_gain: float32 [1024], replicated
- grad_w_gate: float32 [1024, 3072], P('dp', 'tensor')
- grad_w_up: float32 [1024, 3072], P('dp', 'tensor')
- grad_w_down: float32 [3072, 1024], P('tensor', 'dp')
The draws below stay inside these ranges and needn't reach their ends.
Inputs may be any that keep to these rules, and one draw needn't show every extreme that they name: `segment_ids`: within each sequence the segment numbers start at 0, never fall, and each document holds 1 to 336 tokens.
All inputs are finite; a program needn't handle non-finite values.
Results may differ from the reference program's by a relative error of at most 0.023.
Values may be sent and summed in bfloat16 or wider, within the bound.
A program may use at most 128 MiB of HBM per device.

```python
import math
import jax
import jax.numpy as jnp
import numpy as np
from jax import lax

MODEL_WIDTH = 1024
HQ = 16
KEY_VALUE_HEADS = 8
HEAD_SIZE = 128
FF = 3072
LEN = 448
DOCS = 3
DOC_MOST = 336
SEQS = 16
TOKENS = 7168


def with_spikes(result, stream_key, source, target, blocks, factor):
    def block_of(dim):
        return (jnp.arange(result.shape[dim]) // (result.shape[dim] // blocks)).reshape((-1,) + (1,) * (result.ndim - 1 - dim))

    near = jax.random.permutation(stream_key, blocks)[block_of(target)]
    far = (block_of(target) + blocks // 2) % blocks
    return jnp.where((block_of(source) == near) | (block_of(source) == far), factor * result, result)


def block_levels(key, extent, shards, low, high):
    def one(axis_at, shards_of):
        heights = jax.random.uniform(jax.random.fold_in(jax.random.fold_in(key, 6), axis_at), (shards_of,), jnp.float32, low / len(shards), high / len(shards))
        return jnp.repeat(jnp.exp(heights), extent[axis_at] // shards_of).reshape((-1,) + (1,) * (len(extent) - axis_at - 1))

    level = one(*shards[0])
    for cut in shards[1:]:
        level = level * one(*cut)
    return level


def profile(count, total, reach, skew):
    weights = [(1 << 20) // math.isqrt(standing ** skew) + 1 for standing in range(2, count + 1)]
    spare, given = total - reach - (count - 1), [1] * (count - 1)
    while spare > 0:
        free = [i for i in range(count - 1) if given[i] < reach]
        whole, left = sum([weights[i] for i in free]), spare
        for i in free:
            extra = min(reach - given[i], max(1, left * weights[i] // whole), spare)
            given[i] = given[i] + extra
            spare = spare - extra
    return np.array([reach] + given)


def uneven(stream_key, count, total, reach, slope):
    if count == 2:
        one = jax.random.randint(stream_key, (), max(1, total - reach), min(reach, total - 1) + 1)
        return jnp.stack([one, total - one])
    sizes = jnp.asarray(profile(count, total, reach, slope), jnp.int32)
    pairs = (count - 1) // 2
    source_of, sink = sizes[1:1 + 2 * pairs:2], sizes[2:2 + 2 * pairs:2]
    room = jnp.minimum(source_of - 1, reach - sink)
    moved = jax.random.randint(jax.random.fold_in(stream_key, 1), (pairs,), 0, 1 << 20) % (room + 1)
    sizes = sizes.at[1:1 + 2 * pairs:2].set(source_of - moved).at[2:2 + 2 * pairs:2].set(sink + moved)
    return sizes[jax.random.permutation(jax.random.fold_in(stream_key, 2), count)]


def noise(own_key, shape, width, bound, split=(), held_as=jnp.bfloat16):
    level = block_levels(own_key, shape, split, -0.22, 0.18) if split else 1.0
    array = jax.random.normal(own_key, shape, jnp.float32) * width * level
    return jnp.minimum(jnp.maximum(array, -bound), bound).astype(held_as)


def bell_draw_with(rng, extent, width, reach, pieces, heavy, kind=jnp.bfloat16):
    entries = width * jax.random.normal(rng, extent, jnp.float32)
    if pieces:
        entries = entries * block_levels(rng, extent, pieces, -0.22, 0.18)
    return jnp.clip(with_spikes(entries, jax.random.fold_in(rng, 3), *heavy), -reach, reach).astype(kind)


def setup_inputs(seed: int = 0) -> dict:
    key_list = jax.random.split(jax.random.key(seed), 15)
    return {
        "hidden_in": bell_draw_with(key_list[0], (TOKENS, MODEL_WIDTH), 1.0, 6.0, ((0, 16),), (0, 1, 16, 2.0)),
        "segment_ids": jax.vmap(lambda own: jnp.searchsorted(jnp.cumsum(uneven(own, DOCS, LEN, DOC_MOST, 0)), jnp.arange(LEN), side="right"))(jax.random.split(key_list[1], SEQS)).reshape((SEQS, LEN)).astype(jnp.int32),
        "attn_gain": jnp.clip(jax.random.uniform(key_list[2], (MODEL_WIDTH,), jnp.float32, 0.5, 1.5), 0.5, 1.5),
        "w_query": noise(key_list[3], (MODEL_WIDTH, HQ * HEAD_SIZE), MODEL_WIDTH ** -0.5, 0.1875, ((1, 2),)),
        "key_projection": noise(key_list[4], (MODEL_WIDTH, KEY_VALUE_HEADS * HEAD_SIZE), MODEL_WIDTH ** -0.5, 0.1875, ((1, 2),)),
        "value_projection": noise(key_list[5], (MODEL_WIDTH, KEY_VALUE_HEADS * HEAD_SIZE), MODEL_WIDTH ** -0.5, 0.1875, ((1, 2),)),
        "query_gain": jnp.clip(jnp.exp(jax.random.uniform(key_list[6], (HEAD_SIZE,), jnp.float32, math.log(0.5), math.log(2.0))), 0.5, 2.0),
        "key_gain": jnp.clip(jnp.exp(jax.random.uniform(key_list[7], (HEAD_SIZE,), jnp.float32, math.log(0.5), math.log(2.0))), 0.5, 2.0),
        "w_out": noise(key_list[8], (HQ * HEAD_SIZE, MODEL_WIDTH), (HQ * HEAD_SIZE // 64) ** -0.5, 1.0, ((0, 2),)),
        "mlp_gain": jnp.clip(jax.random.uniform(key_list[9], (MODEL_WIDTH,), jnp.float32, 0.5, 1.5), 0.5, 1.5),
        "w_gate": noise(key_list[10], (MODEL_WIDTH, FF), MODEL_WIDTH ** -0.5, 0.1875, ((1, 2),)),
        "w_up": noise(key_list[11], (MODEL_WIDTH, FF), MODEL_WIDTH ** -0.5, 0.1875, ((1, 2),)),
        "w_down": noise(key_list[12], (FF, MODEL_WIDTH), (FF // 4) ** -0.5, 0.21875, ((0, 2),)),
        "cotangent": bell_draw_with(key_list[13], (TOKENS, MODEL_WIDTH), 1.0, 6.0, ((0, 32),), (0, 1, 32, 2.75)),
    }


EPS = 1e-06
THETA = 1000000.0

def rms_scale(values):
    return lax.rsqrt(lax.optimization_barrier(jnp.mean(values * values, axis=-1, keepdims=True)) + EPS)

def norm_backward(grad_normed, normed, scale_rows, gain):
    weighted = grad_normed * gain
    return scale_rows * (weighted - normed * lax.optimization_barrier(jnp.mean(weighted * normed, axis=-1, keepdims=True)))

def rotate_half(values):
    middle = values.shape[-1] // 2
    return jnp.concatenate([-values[..., middle:], values[..., :middle]], axis=-1)

def rope_tables(length, head_width, dtype):
    middle = head_width // 2
    inverse = THETA ** (-(jnp.arange(middle).astype(dtype) * 2.0 / head_width))
    angles = jnp.arange(length).astype(dtype)[:, None] * inverse[None, :]
    angles = jnp.concatenate([angles, angles], axis=-1)
    return (jnp.cos(angles), jnp.sin(angles))

def attention_mask(segment):
    length = segment.shape[0]
    query_place = jnp.arange(length)[:, None]
    key_place = jnp.arange(length)[None, :]
    return (key_place <= query_place) & (segment[:, None] == segment[None, :])

def attend_scores(query_rot, key_rot, segment):
    length, head_count, head_width = query_rot.shape
    group_count = key_rot.shape[1]
    repeat = head_count // group_count
    factor = head_width ** (-0.5)
    grouped = query_rot.reshape(length, group_count, repeat, head_width).astype(jnp.float32)
    scores = jnp.einsum('qgrd,kgd->grqk', grouped, key_rot.astype(jnp.float32)) * factor
    scores = jnp.where(attention_mask(segment), scores, -1e+30)
    return (grouped, scores, factor)

def attend_forward(query_rot, key_rot, value_low, segment):
    length, head_count, head_width = query_rot.shape
    grouped, scores, factor = attend_scores(query_rot, key_rot, segment)
    highest = lax.optimization_barrier(jnp.max(scores, axis=-1, keepdims=True))
    log_total = highest + jnp.log(lax.optimization_barrier(jnp.sum(jnp.exp(scores - highest), axis=-1, keepdims=True)))
    soft_low = jnp.exp(scores - log_total).astype(jnp.bfloat16)
    attended = jnp.einsum('grqk,kgd->qgrd', soft_low.astype(jnp.float32), value_low.astype(jnp.float32))
    return (attended.reshape(length, head_count * head_width).astype(jnp.bfloat16), log_total)

def attend_backward(query_rot, key_rot, value_low, segment, log_total, attended, grad_attended):
    length, head_count, head_width = query_rot.shape
    group_count = key_rot.shape[1]
    repeat = head_count // group_count
    grouped, scores, factor = attend_scores(query_rot, key_rot, segment)
    soft_wide = jnp.exp(scores - log_total)
    soft_low = soft_wide.astype(jnp.bfloat16)
    grad_grouped = grad_attended.reshape(length, group_count, repeat, head_width)
    grad_low = grad_grouped.astype(jnp.bfloat16)
    old_grouped = attended.reshape(length, group_count, repeat, head_width).astype(jnp.float32)
    delta_rows = jnp.transpose(lax.optimization_barrier(jnp.sum(grad_grouped * old_grouped, axis=-1)), (1, 2, 0))[..., None]
    grad_soft = jnp.einsum('qgrd,kgd->grqk', grad_low.astype(jnp.float32), value_low.astype(jnp.float32))
    grad_scores = (soft_wide * (grad_soft - delta_rows) * factor).astype(jnp.bfloat16)
    grad_query = jnp.einsum('grqk,kgd->qgrd', grad_scores.astype(jnp.float32), key_rot.astype(jnp.float32))
    grad_key = jnp.einsum('grqk,qgrd->kgd', grad_scores.astype(jnp.float32), grouped)
    grad_value = jnp.einsum('grqk,qgrd->kgd', soft_low.astype(jnp.float32), grad_low.astype(jnp.float32))
    return (grad_query.reshape(length, head_count, head_width), grad_key, grad_value)

def matmul(left, right):
    return jnp.dot(left, right, preferred_element_type=jnp.float32)

def one_sequence(weights, hidden_in, segment, cotangent):
    attn_gain, w_query, key_projection, value_projection, query_gain, key_gain, w_out, mlp_gain, w_gate, w_up, w_down = weights
    length = hidden_in.shape[0]
    head_width = query_gain.shape[0]
    cosine, sine = rope_tables(length, head_width, jnp.float32)
    cosine = cosine[:, None, :]
    sine = sine[:, None, :]
    hidden_wide = hidden_in.astype(jnp.float32)
    scale_one = rms_scale(hidden_wide)
    normed_one = hidden_wide * scale_one
    input_one = (normed_one * attn_gain).astype(jnp.bfloat16)
    query_raw = matmul(input_one, w_query).reshape(length, -1, head_width)
    key_raw = matmul(input_one, key_projection).reshape(length, -1, head_width)
    value_low = matmul(input_one, value_projection).astype(jnp.bfloat16).reshape(length, -1, head_width)
    query_scale = rms_scale(query_raw)
    query_unit = query_raw * query_scale
    query_normed = query_unit * query_gain
    query_rot = (query_normed * cosine + rotate_half(query_normed) * sine).astype(jnp.bfloat16)
    key_scale = rms_scale(key_raw)
    key_unit = key_raw * key_scale
    key_normed = key_unit * key_gain
    key_rot = (key_normed * cosine + rotate_half(key_normed) * sine).astype(jnp.bfloat16)
    attended, log_total = attend_forward(query_rot, key_rot, value_low, segment)
    middle = hidden_wide + matmul(attended, w_out)
    scale_two = rms_scale(middle)
    normed_two = middle * scale_two
    input_two = (normed_two * mlp_gain).astype(jnp.bfloat16)
    gate = matmul(input_two, w_gate)
    up_part = matmul(input_two, w_up)
    gate_sig = jax.nn.sigmoid(gate)
    swish = gate * gate_sig
    hidden_units = (swish * up_part).astype(jnp.bfloat16)
    layer_output = (middle + matmul(hidden_units, w_down)).astype(jnp.bfloat16)
    grad_w_down = matmul(hidden_units.T, cotangent)
    grad_hidden = matmul(cotangent, w_down.T)
    grad_gate_in = (grad_hidden * up_part * gate_sig * (1.0 + gate * (1.0 - gate_sig))).astype(jnp.bfloat16)
    up_input_gradient = (grad_hidden * swish).astype(jnp.bfloat16)
    grad_w_gate = matmul(input_two.T, grad_gate_in)
    grad_w_up = matmul(input_two.T, up_input_gradient)
    grad_input_two = matmul(grad_gate_in, w_gate.T) + matmul(up_input_gradient, w_up.T)
    grad_mlp_gain = lax.optimization_barrier(jnp.sum(grad_input_two * normed_two, axis=0))
    grad_middle = cotangent.astype(jnp.float32) + norm_backward(grad_input_two, normed_two, scale_two, mlp_gain)
    grad_middle_low = grad_middle.astype(jnp.bfloat16)
    grad_w_out = matmul(attended.T, grad_middle_low)
    grad_attended = matmul(grad_middle_low, w_out.T)
    grad_query_rot, grad_key_rot, grad_value = attend_backward(query_rot, key_rot, value_low, segment, log_total, attended, grad_attended)
    grad_query_normed = grad_query_rot * cosine - rotate_half(grad_query_rot * sine)
    grad_key_normed = grad_key_rot * cosine - rotate_half(grad_key_rot * sine)
    grad_query_gain = lax.optimization_barrier(jnp.sum(grad_query_normed * query_unit, axis=(0, 1)))
    grad_key_gain = lax.optimization_barrier(jnp.sum(grad_key_normed * key_unit, axis=(0, 1)))
    grad_query_low = norm_backward(grad_query_normed, query_unit, query_scale, query_gain).reshape(length, -1).astype(jnp.bfloat16)
    grad_key_low = norm_backward(grad_key_normed, key_unit, key_scale, key_gain).reshape(length, -1).astype(jnp.bfloat16)
    grad_value_low = grad_value.reshape(length, -1).astype(jnp.bfloat16)
    grad_w_query = matmul(input_one.T, grad_query_low)
    grad_w_key = matmul(input_one.T, grad_key_low)
    grad_w_value = matmul(input_one.T, grad_value_low)
    grad_input_one = matmul(grad_query_low, w_query.T) + matmul(grad_key_low, key_projection.T) + matmul(grad_value_low, value_projection.T)
    attention_gain_gradient = lax.optimization_barrier(jnp.sum(grad_input_one * normed_one, axis=0))
    grad_in = grad_middle + norm_backward(grad_input_one, normed_one, scale_one, attn_gain)
    grads = (attention_gain_gradient, grad_w_query, grad_w_key, grad_w_value, grad_query_gain, grad_key_gain, grad_w_out, grad_mlp_gain, grad_w_gate, grad_w_up, grad_w_down)
    return (layer_output, grad_in, grads)

def reference(hidden_in, segment_ids, attn_gain, w_query, key_projection, value_projection, query_gain, key_gain, w_out, mlp_gain, w_gate, w_up, w_down, cotangent):
    weights = (attn_gain, w_query, key_projection, value_projection, query_gain, key_gain, w_out, mlp_gain, w_gate, w_up, w_down)
    seq_count = segment_ids.shape[0]
    inputs_seq = hidden_in.reshape(seq_count, LEN, MODEL_WIDTH)
    cot_seq = cotangent.reshape(seq_count, LEN, MODEL_WIDTH)
    initial = tuple((jnp.zeros(weight.shape, jnp.float32) for weight in weights))

    def advance(carry, item):
        layer_output, grad_in, grads = one_sequence(weights, item[0], item[1], item[2])
        return (tuple((total + grad for total, grad in zip(carry, grads))), (layer_output, grad_in))
    totals, results = lax.scan(advance, initial, (inputs_seq, segment_ids, cot_seq))
    return (results[0].reshape(-1, MODEL_WIDTH), results[1].reshape(-1, MODEL_WIDTH), totals[0], totals[1], totals[2], totals[3], totals[4], totals[5], totals[6], totals[7], totals[8], totals[9], totals[10])
```

```python
import functools

import jax
import jax.numpy as jnp
from jax import lax
from jax.sharding import PartitionSpec as P

EPS = 1e-06
THETA = 1000000.0


def rms_scale(values):
    return lax.rsqrt(jnp.mean(values * values, axis=-1, keepdims=True) + EPS)


def norm_backward(grad_normed, normed, scale_rows, gain):
    weighted = grad_normed * gain
    return scale_rows * (weighted - normed * jnp.mean(weighted * normed, axis=-1, keepdims=True))


def rotate_half(values):
    middle = values.shape[-1] // 2
    return jnp.concatenate([-values[..., middle:], values[..., :middle]], axis=-1)


def rope_tables(length, head_width, dtype):
    middle = head_width // 2
    inverse = THETA ** (-(jnp.arange(middle).astype(dtype) * 2.0 / head_width))
    angles = jnp.arange(length).astype(dtype)[:, None] * inverse[None, :]
    angles = jnp.concatenate([angles, angles], axis=-1)
    return (jnp.cos(angles), jnp.sin(angles))


def attention_mask(segment):
    length = segment.shape[0]
    query_place = jnp.arange(length)[:, None]
    key_place = jnp.arange(length)[None, :]
    return (key_place <= query_place) & (segment[:, None] == segment[None, :])


def matmul(left, right):
    return jnp.dot(left, right, preferred_element_type=jnp.float32)


def contract_first(left, right):
    return lax.dot_general(
        left, right, (((0,), (0,)), ((), ())), preferred_element_type=jnp.float32
    )


def contract_last(left, right):
    return lax.dot_general(
        left, right, (((1,), (1,)), ((), ())), preferred_element_type=jnp.float32
    )


def attend_scores(query_rot, key_rot, segment):
    length, head_count, head_width = query_rot.shape
    group_count = key_rot.shape[1]
    repeat = head_count // group_count
    factor = head_width ** (-0.5)
    grouped = query_rot.reshape(length, group_count, repeat, head_width)
    scores = (
        jnp.einsum("qgrd,kgd->grqk", grouped, key_rot, preferred_element_type=jnp.float32) * factor
    )
    scores = jnp.where(attention_mask(segment), scores, -1e30)
    return (grouped, scores, factor)


def attend_forward(query_rot, key_rot, value_low, segment):
    length, head_count, head_width = query_rot.shape
    grouped, scores, factor = attend_scores(query_rot, key_rot, segment)
    highest = jnp.max(scores, axis=-1, keepdims=True)
    log_total = highest + jnp.log(jnp.sum(jnp.exp(scores - highest), axis=-1, keepdims=True))
    soft_low = jnp.exp(scores - log_total).astype(jnp.bfloat16)
    attended = jnp.einsum("grqk,kgd->qgrd", soft_low, value_low, preferred_element_type=jnp.float32)
    return (attended.reshape(length, head_count * head_width).astype(jnp.bfloat16), log_total)


def attend_backward(query_rot, key_rot, value_low, segment, log_total, attended, grad_attended):
    length, head_count, head_width = query_rot.shape
    group_count = key_rot.shape[1]
    repeat = head_count // group_count
    grouped, scores, factor = attend_scores(query_rot, key_rot, segment)
    soft_wide = jnp.exp(scores - log_total)
    soft_low = soft_wide.astype(jnp.bfloat16)
    grad_grouped = grad_attended.reshape(length, group_count, repeat, head_width)
    grad_low = grad_grouped.astype(jnp.bfloat16)
    old_grouped = attended.reshape(length, group_count, repeat, head_width).astype(jnp.float32)
    delta_rows = jnp.transpose(jnp.sum(grad_grouped * old_grouped, axis=-1), (1, 2, 0))[..., None]
    grad_soft = jnp.einsum(
        "qgrd,kgd->grqk", grad_low, value_low, preferred_element_type=jnp.float32
    )
    grad_scores = (soft_wide * (grad_soft - delta_rows) * factor).astype(jnp.bfloat16)
    grad_query = jnp.einsum(
        "grqk,kgd->qgrd", grad_scores, key_rot, preferred_element_type=jnp.float32
    )
    grad_key = jnp.einsum(
        "grqk,qgrd->kgd", grad_scores, grouped, preferred_element_type=jnp.float32
    )
    grad_value = jnp.einsum(
        "grqk,qgrd->kgd", soft_low, grad_low, preferred_element_type=jnp.float32
    )
    return (grad_query.reshape(length, head_count, head_width), grad_key, grad_value)


def swap(values, axis, count, flip):
    return lax.ppermute(values, axis, [(d, d ^ flip) for d in range(count)])


def pair_sum(values, count):
    low = values.astype(jnp.bfloat16)
    if count != 2:
        return lax.psum(low, "tensor").astype(jnp.float32)
    return low.astype(jnp.float32) + swap(low, "tensor", 2, 1).astype(jnp.float32)


def pair_scatter(values, count):
    if count != 2:
        return lax.psum_scatter(
            values.astype(jnp.bfloat16), "tensor", scatter_dimension=0, tiled=True
        ).astype(jnp.float32)
    mine = lax.axis_index("tensor")
    rows = values.shape[0] // 2
    sent = lax.dynamic_slice_in_dim(values, (1 - mine) * rows, rows, 0).astype(jnp.bfloat16)
    kept = lax.dynamic_slice_in_dim(values, mine * rows, rows, 0)
    return kept + swap(sent, "tensor", 2, 1).astype(jnp.float32)


def pair_gather(values, count):
    if count != 2:
        return lax.all_gather(values, "tensor", axis=0, tiled=True)
    other = swap(values, "tensor", 2, 1)
    first = lax.axis_index("tensor") == 0
    return jnp.concatenate(
        [jnp.where(first, values, other), jnp.where(first, other, values)], axis=0
    )


def halving_scatter(values, count, order):
    bits = count.bit_length() - 1
    share = values.shape[0] // count
    columns = values.shape[1]
    total = values.astype(jnp.bfloat16)
    place = lax.axis_index("dp")
    left = list(range(bits))[::-1]
    for bit in order:
        at = left.index(bit)
        outer = 2**at
        inner = 2 ** (len(left) - 1 - at) * share
        split = total.reshape(outer, 2, inner, columns)
        own = (place >> bit) & 1
        kept = lax.dynamic_index_in_dim(split, own, 1, keepdims=False)
        sent = lax.dynamic_index_in_dim(split, 1 - own, 1, keepdims=False)
        got = swap(sent, "dp", count, 1 << bit)
        wide = kept.astype(jnp.float32) + got.astype(jnp.float32)
        left.remove(bit)
        total = wide.astype(jnp.bfloat16) if left else wide
    return total.reshape(share, columns)


def doubling_sum(values, dp_count, tensor_count):
    flip = 1
    while flip < tensor_count:
        values = values + swap(values, "tensor", tensor_count, flip)
        flip *= 2
    flip = 1
    while flip < dp_count:
        values = values + swap(values, "dp", dp_count, flip)
        flip *= 2
    return values


def on_device(
    dp_count,
    tensor_count,
    hidden_in,
    segment_ids,
    attn_gain,
    w_query,
    key_projection,
    value_projection,
    query_gain,
    key_gain,
    w_out,
    mlp_gain,
    w_gate,
    w_up,
    w_down,
    cotangent,
):
    seq_count = segment_ids.shape[0]
    length = segment_ids.shape[1]
    token_count = hidden_in.shape[0]
    head_width = query_gain.shape[0]
    share_rows = cotangent.shape[0]
    start_row = lax.axis_index("tensor") * share_rows
    bits = dp_count.bit_length() - 1
    order_a = list(range(bits))
    order_b = [0] + list(range(2, bits)) + ([1] if bits > 1 else [])
    cot_all = pair_gather(cotangent, tensor_count)
    cosine, sine = rope_tables(length, head_width, jnp.float32)
    cosine = cosine[:, None, :]
    sine = sine[:, None, :]
    hidden_wide = hidden_in.astype(jnp.float32)
    scale_one = rms_scale(hidden_wide)
    normed_one = hidden_wide * scale_one
    input_one = (normed_one * attn_gain).astype(jnp.bfloat16)
    query_raw = matmul(input_one, w_query).reshape(seq_count, length, -1, head_width)
    key_raw = matmul(input_one, key_projection).reshape(seq_count, length, -1, head_width)
    value_low = (
        matmul(input_one, value_projection)
        .astype(jnp.bfloat16)
        .reshape(seq_count, length, -1, head_width)
    )
    query_scale = rms_scale(query_raw)
    query_unit = query_raw * query_scale
    query_normed = query_unit * query_gain
    query_rot = (query_normed * cosine + rotate_half(query_normed) * sine).astype(jnp.bfloat16)
    key_scale = rms_scale(key_raw)
    key_unit = key_raw * key_scale
    key_normed = key_unit * key_gain
    key_rot = (key_normed * cosine + rotate_half(key_normed) * sine).astype(jnp.bfloat16)

    def forward_one(items):
        return attend_forward(items[0], items[1], items[2], items[3])

    attended, log_total = lax.map(forward_one, (query_rot, key_rot, value_low, segment_ids))
    attended_flat = attended.reshape(token_count, -1)
    attn_part = matmul(attended_flat, w_out)
    attn_total = pair_sum(attn_part, tensor_count)
    middle = hidden_wide + attn_total
    scale_two = rms_scale(middle)
    normed_two = middle * scale_two
    input_two = (normed_two * mlp_gain).astype(jnp.bfloat16)
    middle_rows = lax.dynamic_slice_in_dim(middle, start_row, share_rows, 0)
    gate = matmul(input_two, w_gate)
    up_part = matmul(input_two, w_up)
    gate_sig = jax.nn.sigmoid(gate)
    swish = gate * gate_sig
    hidden_units = (swish * up_part).astype(jnp.bfloat16)
    mlp_rows = pair_scatter(matmul(hidden_units, w_down), tensor_count)
    layer_output = (middle_rows + mlp_rows).astype(jnp.bfloat16)
    grad_down = contract_first(cot_all, hidden_units)
    grad_down_rows = halving_scatter(grad_down, dp_count, order_a)
    grad_hidden = contract_last(cot_all, w_down)
    grad_gate_in = (grad_hidden * up_part * gate_sig * (1.0 + gate * (1.0 - gate_sig))).astype(
        jnp.bfloat16
    )
    up_input_gradient = (grad_hidden * swish).astype(jnp.bfloat16)
    grad_gate = contract_first(input_two, grad_gate_in)
    grad_up = contract_first(input_two, up_input_gradient)
    grad_gate_rows = halving_scatter(grad_gate, dp_count, order_b)
    grad_up_rows = halving_scatter(grad_up, dp_count, order_a)
    grad_input_two = contract_last(grad_gate_in, w_gate) + contract_last(up_input_gradient, w_up)
    mlp_gain_part = jnp.sum(grad_input_two * normed_two, axis=0)
    back_part = norm_backward(grad_input_two, normed_two, scale_two, mlp_gain)
    grad_middle = cot_all.astype(jnp.float32) + pair_sum(back_part, tensor_count)
    grad_middle_rows = lax.dynamic_slice_in_dim(grad_middle, start_row, share_rows, 0)
    grad_middle_low = grad_middle.astype(jnp.bfloat16)
    grad_out = contract_first(grad_middle_low, attended_flat)
    grad_attended = contract_last(grad_middle_low, w_out).reshape(seq_count, length, -1)

    def backward_one(items):
        return attend_backward(items[0], items[1], items[2], items[3], items[4], items[5], items[6])

    grad_query_rot, grad_key_rot, grad_value = lax.map(
        backward_one,
        (query_rot, key_rot, value_low, segment_ids, log_total, attended, grad_attended),
    )
    grad_query_normed = grad_query_rot * cosine - rotate_half(grad_query_rot * sine)
    grad_key_normed = grad_key_rot * cosine - rotate_half(grad_key_rot * sine)
    query_gain_part = jnp.sum(grad_query_normed * query_unit, axis=(0, 1, 2))
    key_gain_part = jnp.sum(grad_key_normed * key_unit, axis=(0, 1, 2))
    grad_query_low = (
        norm_backward(grad_query_normed, query_unit, query_scale, query_gain)
        .reshape(token_count, -1)
        .astype(jnp.bfloat16)
    )
    grad_key_low = (
        norm_backward(grad_key_normed, key_unit, key_scale, key_gain)
        .reshape(token_count, -1)
        .astype(jnp.bfloat16)
    )
    grad_value_low = grad_value.reshape(token_count, -1).astype(jnp.bfloat16)
    grad_query_weight = contract_first(input_one, grad_query_low)
    grad_key_weight = contract_first(input_one, grad_key_low)
    grad_value_weight = contract_first(input_one, grad_value_low)
    grad_input_one = (
        contract_last(grad_query_low, w_query)
        + contract_last(grad_key_low, key_projection)
        + contract_last(grad_value_low, value_projection)
    )
    grad_one_rows = pair_scatter(grad_input_one, tensor_count)
    normed_rows = lax.dynamic_slice_in_dim(normed_one, start_row, share_rows, 0)
    scale_rows = lax.dynamic_slice_in_dim(scale_one, start_row, share_rows, 0)
    attn_gain_part = jnp.sum(grad_one_rows * normed_rows, axis=0)
    grad_in = grad_middle_rows + norm_backward(grad_one_rows, normed_rows, scale_rows, attn_gain)
    grad_out_rows = halving_scatter(grad_out, dp_count, order_b)
    grad_key_value_rows = halving_scatter(
        jnp.concatenate([grad_key_weight, grad_value_weight], axis=1), dp_count, order_b
    )
    grad_query_rows = halving_scatter(grad_query_weight, dp_count, order_a)
    key_columns = grad_key_weight.shape[1]
    row_sums = (
        grad_query_rows,
        grad_key_value_rows[:, :key_columns],
        grad_key_value_rows[:, key_columns:],
        grad_gate_rows,
        grad_up_rows,
    )
    column_sums = (grad_out_rows.T, grad_down_rows.T)
    gains = doubling_sum(
        jnp.concatenate([attn_gain_part, mlp_gain_part, query_gain_part, key_gain_part]),
        dp_count,
        tensor_count,
    )
    width = attn_gain_part.shape[0]
    gain_totals = (
        gains[:width],
        gains[2 * width : 2 * width + head_width],
        gains[2 * width + head_width :],
        gains[width : 2 * width],
    )
    return (
        layer_output,
        grad_in,
        gain_totals[0],
        row_sums[0],
        row_sums[1],
        row_sums[2],
        gain_totals[1],
        gain_totals[2],
        column_sums[0],
        gain_totals[3],
        row_sums[3],
        row_sums[4],
        column_sums[1],
    )


def solution(mesh):
    placed = (
        P("dp", None),
        P("dp", None),
        P(),
        P(None, "tensor"),
        P(None, "tensor"),
        P(None, "tensor"),
        P(),
        P(),
        P("tensor", None),
        P(),
        P(None, "tensor"),
        P(None, "tensor"),
        P("tensor", None),
        P(("dp", "tensor"), None),
    )
    return jax.shard_map(
        functools.partial(on_device, mesh.shape["dp"], mesh.shape["tensor"]),
        mesh=mesh,
        in_specs=placed,
        out_specs=(
            P(("dp", "tensor"), None),
            P(("dp", "tensor"), None),
            P(),
            P("dp", "tensor"),
            P("dp", "tensor"),
            P("dp", "tensor"),
            P(),
            P(),
            P("tensor", "dp"),
            P(),
            P("dp", "tensor"),
            P("dp", "tensor"),
            P("tensor", "dp"),
        ),
        check_vma=False,
    )
```

```python
import functools

import jax
import jax.numpy as jnp
from jax import lax
from jax.sharding import PartitionSpec as P

EPS = 1e-06
THETA = 1000000.0


def rms_scale(values):
    return lax.rsqrt(jnp.mean(values * values, axis=-1, keepdims=True) + EPS)


def norm_backward(grad_normed, normed, scale_rows, gain):
    weighted = grad_normed * gain
    return scale_rows * (weighted - normed * jnp.mean(weighted * normed, axis=-1, keepdims=True))


def rotate_half(values):
    middle = values.shape[-1] // 2
    return jnp.concatenate([-values[..., middle:], values[..., :middle]], axis=-1)


def rope_tables(length, head_width, dtype):
    middle = head_width // 2
    inverse = THETA ** (-(jnp.arange(middle).astype(dtype) * 2.0 / head_width))
    angles = jnp.arange(length).astype(dtype)[:, None] * inverse[None, :]
    angles = jnp.concatenate([angles, angles], axis=-1)
    return (jnp.cos(angles), jnp.sin(angles))


def attention_mask(segment):
    length = segment.shape[0]
    query_place = jnp.arange(length)[:, None]
    key_place = jnp.arange(length)[None, :]
    return (key_place <= query_place) & (segment[:, None] == segment[None, :])


def matmul(left, right):
    return jnp.dot(left, right, preferred_element_type=jnp.float32)


def contract_first(left, right):
    return lax.dot_general(
        left, right, (((0,), (0,)), ((), ())), preferred_element_type=jnp.float32
    )


def contract_last(left, right):
    return lax.dot_general(
        left, right, (((1,), (1,)), ((), ())), preferred_element_type=jnp.float32
    )


def attend_scores(query_rot, key_rot, segment):
    length, head_count, head_width = query_rot.shape
    group_count = key_rot.shape[1]
    repeat = head_count // group_count
    factor = head_width ** (-0.5)
    grouped = query_rot.reshape(length, group_count, repeat, head_width)
    scores = (
        jnp.einsum("qgrd,kgd->grqk", grouped, key_rot, preferred_element_type=jnp.float32) * factor
    )
    scores = jnp.where(attention_mask(segment), scores, -1e30)
    return (grouped, scores, factor)


def attend_forward(query_rot, key_rot, value_low, segment):
    length, head_count, head_width = query_rot.shape
    grouped, scores, factor = attend_scores(query_rot, key_rot, segment)
    highest = jnp.max(scores, axis=-1, keepdims=True)
    log_total = highest + jnp.log(jnp.sum(jnp.exp(scores - highest), axis=-1, keepdims=True))
    soft_low = jnp.exp(scores - log_total).astype(jnp.bfloat16)
    attended = jnp.einsum("grqk,kgd->qgrd", soft_low, value_low, preferred_element_type=jnp.float32)
    return (attended.reshape(length, head_count * head_width).astype(jnp.bfloat16), log_total)


def attend_backward(query_rot, key_rot, value_low, segment, log_total, attended, grad_attended):
    length, head_count, head_width = query_rot.shape
    group_count = key_rot.shape[1]
    repeat = head_count // group_count
    grouped, scores, factor = attend_scores(query_rot, key_rot, segment)
    soft_wide = jnp.exp(scores - log_total)
    soft_low = soft_wide.astype(jnp.bfloat16)
    grad_grouped = grad_attended.reshape(length, group_count, repeat, head_width)
    grad_low = grad_grouped.astype(jnp.bfloat16)
    old_grouped = attended.reshape(length, group_count, repeat, head_width).astype(jnp.float32)
    delta_rows = jnp.transpose(jnp.sum(grad_grouped * old_grouped, axis=-1), (1, 2, 0))[..., None]
    grad_soft = jnp.einsum(
        "qgrd,kgd->grqk", grad_low, value_low, preferred_element_type=jnp.float32
    )
    grad_scores = (soft_wide * (grad_soft - delta_rows) * factor).astype(jnp.bfloat16)
    grad_query = jnp.einsum(
        "grqk,kgd->qgrd", grad_scores, key_rot, preferred_element_type=jnp.float32
    )
    grad_key = jnp.einsum(
        "grqk,qgrd->kgd", grad_scores, grouped, preferred_element_type=jnp.float32
    )
    grad_value = jnp.einsum(
        "grqk,qgrd->kgd", soft_low, grad_low, preferred_element_type=jnp.float32
    )
    return (grad_query.reshape(length, head_count, head_width), grad_key, grad_value)


def swap(values, axis, count, flip):
    return lax.ppermute(values, axis, [(d, d ^ flip) for d in range(count)])


def pair_sum(values, count):
    low = values.astype(jnp.bfloat16)
    if count != 2:
        return lax.psum(low, "tensor").astype(jnp.float32)
    return low.astype(jnp.float32) + swap(low, "tensor", 2, 1).astype(jnp.float32)


def pair_scatter(values, count):
    if count != 2:
        return lax.psum_scatter(
            values.astype(jnp.bfloat16), "tensor", scatter_dimension=0, tiled=True
        ).astype(jnp.float32)
    mine = lax.axis_index("tensor")
    rows = values.shape[0] // 2
    sent = lax.dynamic_slice_in_dim(values, (1 - mine) * rows, rows, 0).astype(jnp.bfloat16)
    kept = lax.dynamic_slice_in_dim(values, mine * rows, rows, 0)
    return kept + swap(sent, "tensor", 2, 1).astype(jnp.float32)


def pair_gather(values, count):
    if count != 2:
        return lax.all_gather(values, "tensor", axis=0, tiled=True)
    other = swap(values, "tensor", 2, 1)
    first = lax.axis_index("tensor") == 0
    return jnp.concatenate(
        [jnp.where(first, values, other), jnp.where(first, other, values)], axis=0
    )


def halving_step(state, count):
    total, left, order, share = state
    if not order:
        return state
    bit = order[0]
    place = lax.axis_index("dp")
    columns = total.shape[1]
    at = left.index(bit)
    outer = 2**at
    inner = 2 ** (len(left) - 1 - at) * share
    split = total.reshape(outer, 2, inner, columns)
    own = (place >> bit) & 1
    kept = lax.dynamic_index_in_dim(split, own, 1, keepdims=False)
    sent = lax.dynamic_index_in_dim(split, 1 - own, 1, keepdims=False)
    got = swap(sent, "dp", count, 1 << bit)
    wide = kept.astype(jnp.float32) + got.astype(jnp.float32)
    left = [other for other in left if other != bit]
    total = wide.astype(jnp.bfloat16) if left else wide
    return (total.reshape(outer * inner, columns), left, order[1:], share)


def halving_start(values, count, order):
    bits = count.bit_length() - 1
    low = values.astype(jnp.bfloat16)
    return (low, list(range(bits))[::-1], order, values.shape[0] // count)


def halving_scatter(values, count, order):
    return halving_finish(halving_start(values, count, order), count)


def halving_finish(state, count):
    while state[2]:
        state = halving_step(state, count)
    return state[0].astype(jnp.float32)


def ordered(values, states):
    tied = lax.optimization_barrier((values, [state[0] for state in states]))
    return tied[0], [(total,) + state[1:] for total, state in zip(tied[1], states)]


def doubling_sum(values, dp_count, tensor_count):
    flip = 1
    while flip < tensor_count:
        values = values + swap(values, "tensor", tensor_count, flip)
        flip *= 2
    flip = 1
    while flip < dp_count:
        values = values + swap(values, "dp", dp_count, flip)
        flip *= 2
    return values


def on_device(
    dp_count,
    tensor_count,
    hidden_in,
    segment_ids,
    attn_gain,
    w_query,
    key_projection,
    value_projection,
    query_gain,
    key_gain,
    w_out,
    mlp_gain,
    w_gate,
    w_up,
    w_down,
    cotangent,
):
    seq_count = segment_ids.shape[0]
    length = segment_ids.shape[1]
    token_count = hidden_in.shape[0]
    head_width = query_gain.shape[0]
    share_rows = cotangent.shape[0]
    start_row = lax.axis_index("tensor") * share_rows
    bits = dp_count.bit_length() - 1
    order_a = list(range(bits))
    order_b = [0] + list(range(2, bits)) + ([1] if bits > 1 else [])
    cot_all = pair_gather(cotangent, tensor_count)
    cosine, sine = rope_tables(length, head_width, jnp.float32)
    cosine = cosine[:, None, :]
    sine = sine[:, None, :]
    hidden_wide = hidden_in.astype(jnp.float32)
    scale_one = rms_scale(hidden_wide)
    normed_one = hidden_wide * scale_one
    input_one = (normed_one * attn_gain).astype(jnp.bfloat16)
    query_raw = matmul(input_one, w_query).reshape(seq_count, length, -1, head_width)
    key_raw = matmul(input_one, key_projection).reshape(seq_count, length, -1, head_width)
    value_low = (
        matmul(input_one, value_projection)
        .astype(jnp.bfloat16)
        .reshape(seq_count, length, -1, head_width)
    )
    query_scale = rms_scale(query_raw)
    query_unit = query_raw * query_scale
    query_normed = query_unit * query_gain
    query_rot = (query_normed * cosine + rotate_half(query_normed) * sine).astype(jnp.bfloat16)
    key_scale = rms_scale(key_raw)
    key_unit = key_raw * key_scale
    key_normed = key_unit * key_gain
    key_rot = (key_normed * cosine + rotate_half(key_normed) * sine).astype(jnp.bfloat16)

    def forward_one(items):
        return attend_forward(items[0], items[1], items[2], items[3])

    attended, log_total = lax.map(forward_one, (query_rot, key_rot, value_low, segment_ids))
    attended_flat = attended.reshape(token_count, -1)
    attn_part = matmul(attended_flat, w_out)
    attn_total = pair_sum(attn_part, tensor_count)
    middle = hidden_wide + attn_total
    scale_two = rms_scale(middle)
    normed_two = middle * scale_two
    input_two = (normed_two * mlp_gain).astype(jnp.bfloat16)
    middle_rows = lax.dynamic_slice_in_dim(middle, start_row, share_rows, 0)
    gate = matmul(input_two, w_gate)
    up_part = matmul(input_two, w_up)
    gate_sig = jax.nn.sigmoid(gate)
    swish = gate * gate_sig
    hidden_units = (swish * up_part).astype(jnp.bfloat16)
    mlp_rows = pair_scatter(matmul(hidden_units, w_down), tensor_count)
    layer_output = (middle_rows + mlp_rows).astype(jnp.bfloat16)
    grad_down = contract_first(cot_all, hidden_units)
    down_state = halving_start(grad_down, dp_count, order_a)
    grad_hidden = contract_last(cot_all, w_down)
    grad_gate_in = (grad_hidden * up_part * gate_sig * (1.0 + gate * (1.0 - gate_sig))).astype(
        jnp.bfloat16
    )
    up_input_gradient = (grad_hidden * swish).astype(jnp.bfloat16)
    grad_gate = contract_first(input_two, grad_gate_in)
    grad_up = contract_first(input_two, up_input_gradient)
    gate_state = halving_start(grad_gate, dp_count, order_b)
    up_state = halving_start(grad_up, dp_count, order_a)
    grad_input_two = contract_last(grad_gate_in, w_gate) + contract_last(up_input_gradient, w_up)
    mlp_gain_part = jnp.sum(grad_input_two * normed_two, axis=0)
    back_part = norm_backward(grad_input_two, normed_two, scale_two, mlp_gain)
    grad_middle = cot_all.astype(jnp.float32) + pair_sum(back_part, tensor_count)
    grad_middle_rows = lax.dynamic_slice_in_dim(grad_middle, start_row, share_rows, 0)
    grad_middle_low = grad_middle.astype(jnp.bfloat16)
    states = [halving_step(state, dp_count) for state in (down_state, gate_state, up_state)]
    grad_middle_low, states = ordered(grad_middle_low, states)
    grad_out = contract_first(grad_middle_low, attended_flat)
    grad_attended = contract_last(grad_middle_low, w_out).reshape(seq_count, length, -1)

    def backward_one(items):
        return attend_backward(items[0], items[1], items[2], items[3], items[4], items[5], items[6])

    grad_query_rot, grad_key_rot, grad_value = lax.map(
        backward_one,
        (query_rot, key_rot, value_low, segment_ids, log_total, attended, grad_attended),
    )
    states = [halving_step(state, dp_count) for state in states]
    (grad_query_rot, grad_key_rot, grad_value), states = ordered(
        (grad_query_rot, grad_key_rot, grad_value), states
    )
    grad_query_normed = grad_query_rot * cosine - rotate_half(grad_query_rot * sine)
    grad_key_normed = grad_key_rot * cosine - rotate_half(grad_key_rot * sine)
    query_gain_part = jnp.sum(grad_query_normed * query_unit, axis=(0, 1, 2))
    key_gain_part = jnp.sum(grad_key_normed * key_unit, axis=(0, 1, 2))
    grad_query_low = (
        norm_backward(grad_query_normed, query_unit, query_scale, query_gain)
        .reshape(token_count, -1)
        .astype(jnp.bfloat16)
    )
    grad_key_low = (
        norm_backward(grad_key_normed, key_unit, key_scale, key_gain)
        .reshape(token_count, -1)
        .astype(jnp.bfloat16)
    )
    grad_value_low = grad_value.reshape(token_count, -1).astype(jnp.bfloat16)
    states = [halving_step(state, dp_count) for state in states]
    (grad_query_low, grad_key_low, grad_value_low), states = ordered(
        (grad_query_low, grad_key_low, grad_value_low), states
    )
    grad_query_weight = contract_first(input_one, grad_query_low)
    grad_key_weight = contract_first(input_one, grad_key_low)
    grad_value_weight = contract_first(input_one, grad_value_low)
    grad_input_one = (
        contract_last(grad_query_low, w_query)
        + contract_last(grad_key_low, key_projection)
        + contract_last(grad_value_low, value_projection)
    )
    grad_one_rows = pair_scatter(grad_input_one, tensor_count)
    normed_rows = lax.dynamic_slice_in_dim(normed_one, start_row, share_rows, 0)
    scale_rows = lax.dynamic_slice_in_dim(scale_one, start_row, share_rows, 0)
    attn_gain_part = jnp.sum(grad_one_rows * normed_rows, axis=0)
    grad_in = grad_middle_rows + norm_backward(grad_one_rows, normed_rows, scale_rows, attn_gain)
    grad_out_rows = halving_scatter(grad_out, dp_count, order_b)
    grad_key_value_rows = halving_scatter(
        jnp.concatenate([grad_key_weight, grad_value_weight], axis=1), dp_count, order_b
    )
    grad_query_rows = halving_scatter(grad_query_weight, dp_count, order_a)
    grad_down_rows, grad_gate_rows, grad_up_rows = (
        halving_finish(state, dp_count) for state in states
    )
    key_columns = grad_key_weight.shape[1]
    row_sums = (
        grad_query_rows,
        grad_key_value_rows[:, :key_columns],
        grad_key_value_rows[:, key_columns:],
        grad_gate_rows,
        grad_up_rows,
    )
    column_sums = (grad_out_rows.T, grad_down_rows.T)
    gains = doubling_sum(
        jnp.concatenate([attn_gain_part, mlp_gain_part, query_gain_part, key_gain_part]),
        dp_count,
        tensor_count,
    )
    width = attn_gain_part.shape[0]
    gain_totals = (
        gains[:width],
        gains[2 * width : 2 * width + head_width],
        gains[2 * width + head_width :],
        gains[width : 2 * width],
    )
    return (
        layer_output,
        grad_in,
        gain_totals[0],
        row_sums[0],
        row_sums[1],
        row_sums[2],
        gain_totals[1],
        gain_totals[2],
        column_sums[0],
        gain_totals[3],
        row_sums[3],
        row_sums[4],
        column_sums[1],
    )


def solution(mesh):
    placed = (
        P("dp", None),
        P("dp", None),
        P(),
        P(None, "tensor"),
        P(None, "tensor"),
        P(None, "tensor"),
        P(),
        P(),
        P("tensor", None),
        P(),
        P(None, "tensor"),
        P(None, "tensor"),
        P("tensor", None),
        P(("dp", "tensor"), None),
    )
    return jax.shard_map(
        functools.partial(on_device, mesh.shape["dp"], mesh.shape["tensor"]),
        mesh=mesh,
        in_specs=placed,
        out_specs=(
            P(("dp", "tensor"), None),
            P(("dp", "tensor"), None),
            P(),
            P("dp", "tensor"),
            P("dp", "tensor"),
            P("dp", "tensor"),
            P(),
            P(),
            P("tensor", "dp"),
            P(),
            P("dp", "tensor"),
            P("dp", "tensor"),
            P("tensor", "dp"),
        ),
        check_vma=False,
    )
```

```python
import functools

import jax
import jax.numpy as jnp
from jax import lax
from jax.sharding import PartitionSpec as P

EPS = 1e-06
THETA = 1000000.0


def rms_scale(values):
    return lax.rsqrt(jnp.mean(values * values, axis=-1, keepdims=True) + EPS)


def norm_backward(grad_normed, normed, scale_rows, gain):
    weighted = grad_normed * gain
    return scale_rows * (weighted - normed * jnp.mean(weighted * normed, axis=-1, keepdims=True))


def rotate_half(values):
    middle = values.shape[-1] // 2
    return jnp.concatenate([-values[..., middle:], values[..., :middle]], axis=-1)


def rope_tables(length, head_width, dtype):
    middle = head_width // 2
    inverse = THETA ** (-(jnp.arange(middle).astype(dtype) * 2.0 / head_width))
    angles = jnp.arange(length).astype(dtype)[:, None] * inverse[None, :]
    angles = jnp.concatenate([angles, angles], axis=-1)
    return (jnp.cos(angles), jnp.sin(angles))


def attention_mask(segment):
    length = segment.shape[0]
    query_place = jnp.arange(length)[:, None]
    key_place = jnp.arange(length)[None, :]
    return (key_place <= query_place) & (segment[:, None] == segment[None, :])


def matmul(left, right):
    return jnp.dot(left, right, preferred_element_type=jnp.float32)


def contract_first(left, right):
    return lax.dot_general(
        left, right, (((0,), (0,)), ((), ())), preferred_element_type=jnp.float32
    )


def contract_last(left, right):
    return lax.dot_general(
        left, right, (((1,), (1,)), ((), ())), preferred_element_type=jnp.float32
    )


def attend_scores(query_rot, key_rot, segment):
    length, head_count, head_width = query_rot.shape
    group_count = key_rot.shape[1]
    repeat = head_count // group_count
    factor = head_width ** (-0.5)
    grouped = query_rot.reshape(length, group_count, repeat, head_width)
    scores = (
        jnp.einsum("qgrd,kgd->grqk", grouped, key_rot, preferred_element_type=jnp.float32) * factor
    )
    scores = jnp.where(attention_mask(segment), scores, -1e30)
    return (grouped, scores, factor)


def attend_forward(query_rot, key_rot, value_low, segment):
    length, head_count, head_width = query_rot.shape
    grouped, scores, factor = attend_scores(query_rot, key_rot, segment)
    highest = jnp.max(scores, axis=-1, keepdims=True)
    log_total = highest + jnp.log(jnp.sum(jnp.exp(scores - highest), axis=-1, keepdims=True))
    soft_low = jnp.exp(scores - log_total).astype(jnp.bfloat16)
    attended = jnp.einsum("grqk,kgd->qgrd", soft_low, value_low, preferred_element_type=jnp.float32)
    return (attended.reshape(length, head_count * head_width).astype(jnp.bfloat16), log_total)


def attend_backward(query_rot, key_rot, value_low, segment, log_total, attended, grad_attended):
    length, head_count, head_width = query_rot.shape
    group_count = key_rot.shape[1]
    repeat = head_count // group_count
    grouped, scores, factor = attend_scores(query_rot, key_rot, segment)
    soft_wide = jnp.exp(scores - log_total)
    soft_low = soft_wide.astype(jnp.bfloat16)
    grad_grouped = grad_attended.reshape(length, group_count, repeat, head_width)
    grad_low = grad_grouped.astype(jnp.bfloat16)
    old_grouped = attended.reshape(length, group_count, repeat, head_width).astype(jnp.float32)
    delta_rows = jnp.transpose(jnp.sum(grad_grouped * old_grouped, axis=-1), (1, 2, 0))[..., None]
    grad_soft = jnp.einsum(
        "qgrd,kgd->grqk", grad_low, value_low, preferred_element_type=jnp.float32
    )
    grad_scores = (soft_wide * (grad_soft - delta_rows) * factor).astype(jnp.bfloat16)
    grad_query = jnp.einsum(
        "grqk,kgd->qgrd", grad_scores, key_rot, preferred_element_type=jnp.float32
    )
    grad_key = jnp.einsum(
        "grqk,qgrd->kgd", grad_scores, grouped, preferred_element_type=jnp.float32
    )
    grad_value = jnp.einsum(
        "grqk,qgrd->kgd", soft_low, grad_low, preferred_element_type=jnp.float32
    )
    return (grad_query.reshape(length, head_count, head_width), grad_key, grad_value)


def swap(values, axis, count, flip):
    return lax.ppermute(values, axis, [(d, d ^ flip) for d in range(count)])


def pair_sum(values, count):
    low = values.astype(jnp.bfloat16)
    if count != 2:
        return lax.psum(low, "tensor").astype(jnp.float32)
    return low.astype(jnp.float32) + swap(low, "tensor", 2, 1).astype(jnp.float32)


def pair_scatter(values, count):
    if count != 2:
        return lax.psum_scatter(
            values.astype(jnp.bfloat16), "tensor", scatter_dimension=0, tiled=True
        ).astype(jnp.float32)
    mine = lax.axis_index("tensor")
    rows = values.shape[0] // 2
    sent = lax.dynamic_slice_in_dim(values, (1 - mine) * rows, rows, 0).astype(jnp.bfloat16)
    kept = lax.dynamic_slice_in_dim(values, mine * rows, rows, 0)
    return kept + swap(sent, "tensor", 2, 1).astype(jnp.float32)


def pair_gather(values, count):
    if count != 2:
        return lax.all_gather(values, "tensor", axis=0, tiled=True)
    other = swap(values, "tensor", 2, 1)
    first = lax.axis_index("tensor") == 0
    return jnp.concatenate(
        [jnp.where(first, values, other), jnp.where(first, other, values)], axis=0
    )


def halving_step(state, count):
    total, left, order, share = state
    if not order:
        return state
    bit = order[0]
    place = lax.axis_index("dp")
    columns = total.shape[1]
    at = left.index(bit)
    outer = 2**at
    inner = 2 ** (len(left) - 1 - at) * share
    split = total.reshape(outer, 2, inner, columns)
    own = (place >> bit) & 1
    kept = lax.dynamic_index_in_dim(split, own, 1, keepdims=False)
    sent = lax.dynamic_index_in_dim(split, 1 - own, 1, keepdims=False)
    got = swap(sent, "dp", count, 1 << bit)
    wide = kept.astype(jnp.float32) + got.astype(jnp.float32)
    left = [other for other in left if other != bit]
    total = wide.astype(jnp.bfloat16) if left else wide
    return (total.reshape(outer * inner, columns), left, order[1:], share)


def halving_start(values, count, order):
    bits = count.bit_length() - 1
    low = values.astype(jnp.bfloat16)
    return (low, list(range(bits))[::-1], order, values.shape[0] // count)


def halving_scatter(values, count, order):
    return halving_finish(halving_start(values, count, order), count)


def halving_finish(state, count):
    while state[2]:
        state = halving_step(state, count)
    return state[0].astype(jnp.float32)


def ordered(values, states):
    tied = lax.optimization_barrier((values, [state[0] for state in states]))
    return tied[0], [(total,) + state[1:] for total, state in zip(tied[1], states)]


def doubling_sum(values, dp_count, tensor_count):
    flip = 1
    while flip < tensor_count:
        values = values + swap(values, "tensor", tensor_count, flip)
        flip *= 2
    flip = 1
    while flip < dp_count:
        values = values + swap(values, "dp", dp_count, flip)
        flip *= 2
    return values


def on_device(
    dp_count,
    tensor_count,
    hidden_in,
    segment_ids,
    attn_gain,
    w_query,
    key_projection,
    value_projection,
    query_gain,
    key_gain,
    w_out,
    mlp_gain,
    w_gate,
    w_up,
    w_down,
    cotangent,
):
    seq_count = segment_ids.shape[0]
    length = segment_ids.shape[1]
    token_count = hidden_in.shape[0]
    head_width = query_gain.shape[0]
    share_rows = cotangent.shape[0]
    start_row = lax.axis_index("tensor") * share_rows
    bits = dp_count.bit_length() - 1
    order_a = list(range(bits))
    order_b = [0] + list(range(2, bits)) + ([1] if bits > 1 else [])
    cot_all = pair_gather(cotangent, tensor_count)
    cosine, sine = rope_tables(length, head_width, jnp.float32)
    cosine = cosine[:, None, :]
    sine = sine[:, None, :]
    hidden_wide = hidden_in.astype(jnp.float32)
    scale_one = rms_scale(hidden_wide)
    normed_one = hidden_wide * scale_one
    input_one = (normed_one * attn_gain).astype(jnp.bfloat16)
    query_raw = matmul(input_one, w_query).reshape(seq_count, length, -1, head_width)
    key_raw = matmul(input_one, key_projection).reshape(seq_count, length, -1, head_width)
    value_low = (
        matmul(input_one, value_projection)
        .astype(jnp.bfloat16)
        .reshape(seq_count, length, -1, head_width)
    )
    query_scale = rms_scale(query_raw)
    query_unit = query_raw * query_scale
    query_normed = query_unit * query_gain
    query_rot = (query_normed * cosine + rotate_half(query_normed) * sine).astype(jnp.bfloat16)
    key_scale = rms_scale(key_raw)
    key_unit = key_raw * key_scale
    key_normed = key_unit * key_gain
    key_rot = (key_normed * cosine + rotate_half(key_normed) * sine).astype(jnp.bfloat16)

    def forward_one(items):
        return attend_forward(items[0], items[1], items[2], items[3])

    attended, log_total = lax.map(forward_one, (query_rot, key_rot, value_low, segment_ids))
    attended_flat = attended.reshape(token_count, -1)
    half = token_count // 2
    chunks = (slice(0, half), slice(half, token_count))
    arrived = [pair_sum(matmul(attended_flat[rows], w_out), tensor_count) for rows in chunks]
    pieces = []
    for rows, attn_total in zip(chunks, arrived):
        middle = hidden_wide[rows] + attn_total
        scale_two = rms_scale(middle)
        normed_two = middle * scale_two
        input_two = (normed_two * mlp_gain).astype(jnp.bfloat16)
        gate = matmul(input_two, w_gate)
        up_part = matmul(input_two, w_up)
        gate_sig = jax.nn.sigmoid(gate)
        swish = gate * gate_sig
        hidden_units = (swish * up_part).astype(jnp.bfloat16)
        grad_hidden = contract_last(cot_all[rows], w_down)
        grad_gate_in = (grad_hidden * up_part * gate_sig * (1.0 + gate * (1.0 - gate_sig))).astype(
            jnp.bfloat16
        )
        up_input_gradient = (grad_hidden * swish).astype(jnp.bfloat16)
        grad_input_two = contract_last(grad_gate_in, w_gate) + contract_last(
            up_input_gradient, w_up
        )
        gain_part = jnp.sum(grad_input_two * normed_two, axis=0)
        back_part = norm_backward(grad_input_two, normed_two, scale_two, mlp_gain)
        grad_middle = cot_all[rows].astype(jnp.float32) + pair_sum(back_part, tensor_count)
        pieces.append(
            (middle, input_two, hidden_units, grad_gate_in, up_input_gradient, grad_middle, gain_part)
        )
    middle, input_two, hidden_units, grad_gate_in, up_input_gradient, grad_middle = (
        jnp.concatenate([piece[n] for piece in pieces]) for n in range(6)
    )
    mlp_gain_part = pieces[0][6] + pieces[1][6]
    middle_rows = lax.dynamic_slice_in_dim(middle, start_row, share_rows, 0)
    mlp_rows = pair_scatter(matmul(hidden_units, w_down), tensor_count)
    layer_output = (middle_rows + mlp_rows).astype(jnp.bfloat16)
    down_state = halving_start(contract_first(cot_all, hidden_units), dp_count, order_a)
    gate_state = halving_start(contract_first(input_two, grad_gate_in), dp_count, order_b)
    grad_up = contract_first(input_two, up_input_gradient)
    units = grad_up.shape[1] // 256 * 128
    up_state = halving_start(grad_up[:, :units], dp_count, order_a)
    more_state = halving_start(grad_up[:, units:], dp_count, order_b)
    grad_middle_rows = lax.dynamic_slice_in_dim(grad_middle, start_row, share_rows, 0)
    grad_middle_low = grad_middle.astype(jnp.bfloat16)
    states = [halving_step(state, dp_count) for state in (down_state, gate_state, up_state, more_state)]
    grad_middle_low, states = ordered(grad_middle_low, states)
    grad_out = contract_first(grad_middle_low, attended_flat)
    grad_attended = contract_last(grad_middle_low, w_out).reshape(seq_count, length, -1)

    def backward_one(items):
        return attend_backward(items[0], items[1], items[2], items[3], items[4], items[5], items[6])

    grad_query_rot, grad_key_rot, grad_value = lax.map(
        backward_one,
        (query_rot, key_rot, value_low, segment_ids, log_total, attended, grad_attended),
    )
    states = [halving_step(state, dp_count) for state in states]
    grad_query_normed = grad_query_rot * cosine - rotate_half(grad_query_rot * sine)
    grad_key_normed = grad_key_rot * cosine - rotate_half(grad_key_rot * sine)
    query_gain_part = jnp.sum(grad_query_normed * query_unit, axis=(0, 1, 2))
    key_gain_part = jnp.sum(grad_key_normed * key_unit, axis=(0, 1, 2))
    grad_query_low = (
        norm_backward(grad_query_normed, query_unit, query_scale, query_gain)
        .reshape(token_count, -1)
        .astype(jnp.bfloat16)
    )
    grad_key_low = (
        norm_backward(grad_key_normed, key_unit, key_scale, key_gain)
        .reshape(token_count, -1)
        .astype(jnp.bfloat16)
    )
    grad_value_low = grad_value.reshape(token_count, -1).astype(jnp.bfloat16)
    (grad_query_low, grad_key_low, grad_value_low), states = ordered(
        (grad_query_low, grad_key_low, grad_value_low), states
    )
    grad_query_weight = contract_first(input_one, grad_query_low)
    grad_key_weight = contract_first(input_one, grad_key_low)
    grad_value_weight = contract_first(input_one, grad_value_low)
    grad_input_one = (
        contract_last(grad_query_low, w_query)
        + contract_last(grad_key_low, key_projection)
        + contract_last(grad_value_low, value_projection)
    )
    grad_one_rows = pair_scatter(grad_input_one, tensor_count)
    normed_rows = lax.dynamic_slice_in_dim(normed_one, start_row, share_rows, 0)
    scale_rows = lax.dynamic_slice_in_dim(scale_one, start_row, share_rows, 0)
    attn_gain_part = jnp.sum(grad_one_rows * normed_rows, axis=0)
    grad_in = grad_middle_rows + norm_backward(grad_one_rows, normed_rows, scale_rows, attn_gain)
    grad_out_rows = halving_scatter(grad_out, dp_count, order_b)
    grad_key_value_rows = halving_scatter(
        jnp.concatenate([grad_key_weight, grad_value_weight], axis=1), dp_count, order_b
    )
    grad_query_rows = halving_scatter(grad_query_weight, dp_count, order_a)
    grad_down_rows, grad_gate_rows, up_rows, more_rows = (
        halving_finish(state, dp_count) for state in states
    )
    grad_up_rows = jnp.concatenate([up_rows, more_rows], axis=1)
    key_columns = grad_key_weight.shape[1]
    row_sums = (
        grad_query_rows,
        grad_key_value_rows[:, :key_columns],
        grad_key_value_rows[:, key_columns:],
        grad_gate_rows,
        grad_up_rows,
    )
    column_sums = (grad_out_rows.T, grad_down_rows.T)
    gains = doubling_sum(
        jnp.concatenate([attn_gain_part, mlp_gain_part, query_gain_part, key_gain_part]),
        dp_count,
        tensor_count,
    )
    width = attn_gain_part.shape[0]
    gain_totals = (
        gains[:width],
        gains[2 * width : 2 * width + head_width],
        gains[2 * width + head_width :],
        gains[width : 2 * width],
    )
    return (
        layer_output,
        grad_in,
        gain_totals[0],
        row_sums[0],
        row_sums[1],
        row_sums[2],
        gain_totals[1],
        gain_totals[2],
        column_sums[0],
        gain_totals[3],
        row_sums[3],
        row_sums[4],
        column_sums[1],
    )


def solution(mesh):
    placed = (
        P("dp", None),
        P("dp", None),
        P(),
        P(None, "tensor"),
        P(None, "tensor"),
        P(None, "tensor"),
        P(),
        P(),
        P("tensor", None),
        P(),
        P(None, "tensor"),
        P(None, "tensor"),
        P("tensor", None),
        P(("dp", "tensor"), None),
    )
    return jax.shard_map(
        functools.partial(on_device, mesh.shape["dp"], mesh.shape["tensor"]),
        mesh=mesh,
        in_specs=placed,
        out_specs=(
            P(("dp", "tensor"), None),
            P(("dp", "tensor"), None),
            P(),
            P("dp", "tensor"),
            P("dp", "tensor"),
            P("dp", "tensor"),
            P(),
            P(),
            P("tensor", "dp"),
            P(),
            P("dp", "tensor"),
            P("dp", "tensor"),
            P("tensor", "dp"),
        ),
        check_vma=False,
    )
```
